256 devices in a mesh: grp: 8 (over x, core), tp: 32 (over y, z).
Axes of the slice: x: 4, y: 4, z: 8, core: 2. Of those that a mesh axis runs over, the one named last changes fastest.
Arguments:
- attention_output: bfloat16 [4096, 8192], P('grp', 'tp'), may hold values from -6 to 6
- quantized_weight_codes: bfloat16 [8192, 8192], P('tp'), may hold values from -127 to 127, as said below
- column_scale: float32 [8192], P('tp'), may hold values from 0 to 1
- adapter_down_maps: bfloat16 [512, 64, 8192], P('grp', None, 'tp'), may hold values from -0.0625 to 0.0625
- adapter_up_maps: bfloat16 [512, 64, 8192], P('grp', None, 'tp'), may hold values from -0.75 to 0.75
- owning_group_index: int32 [4096, 1], P('grp'), may hold values from 0 to 7; in each aligned block of 512 rows (0 to 511, 512 to 1023, ...) at most 128 rows name the same one
- token_adapter_slot: int32 [4096], P('grp'), may hold values from 0 to 63
Outputs:
- projected: bfloat16 [4096, 8192], P('grp', 'tp')
The draws below stay inside these ranges and needn't reach their ends.
Inputs may be any that keep to these rules, and one draw needn't show every extreme that they name: `owning_group_index`: among the tokens of one index of grp (aligned blocks of 512 tokens) at most 128 name the same owner, and in some blocks some owner is named by exactly 128 of them. `quantized_weight_codes`: every entry is a whole number.
All inputs are finite; a program needn't handle non-finite values.
Results may differ from the reference program's by a relative error of at most 0.0046.
Values may be sent and summed in bfloat16 or wider, within the bound.
No kernel may reach another device: no remote copies, remote signals or barrier semaphores. Data moves between devices by JAX's collectives and lax.ppermute only.
A program may use at most 128 MiB of HBM per device.

```python
import math
import jax
import jax.numpy as jnp
import numpy as np
from jax import lax

MODEL_WIDTH = 8192
ADAPTER_RANK = 64
TOK_GRP = 512
ADAPT_GRP = 64
TOKENS = 4096
ADAPTER_COUNT = 512
CAP = 128
N_GRP = 8
N_TP = 32


def draw_quantized_weight_codes(key, part):
    key = jax.random.fold_in(key, 11)
    pair_key, code_key = jax.random.split(key)
    pairing = jax.random.permutation(pair_key, N_TP)
    block_of = jnp.arange(MODEL_WIDTH, dtype=jnp.int32) // (MODEL_WIDTH // N_TP)
    paired = pairing[block_of][:, None] == block_of[None, :]
    upper = jnp.where(paired, 128, 32).astype(jnp.int32)
    codes = jax.random.randint(code_key, (MODEL_WIDTH, MODEL_WIDTH), 0, 1 << 20, dtype=jnp.int32)
    codes = codes % (2 * upper - 1) - (upper - 1)
    return codes.astype(jnp.float32).astype(jnp.bfloat16)


def draw_column_scale(key, part):
    key = jax.random.fold_in(key, 23)
    spread = jax.random.uniform(key, (MODEL_WIDTH,), jnp.float32, math.log(0.3), math.log(3.0))
    return jnp.exp(spread) / (25.0 * math.sqrt(MODEL_WIDTH))


def plant(entries, own_key, smallest, high):
    longest = entries.shape.index(max(entries.shape))
    spots = []
    for shift in (0, 1):
        where = [jax.random.randint(jax.random.fold_in(own_key, axis), (), 0, length) for axis, length in enumerate(entries.shape)]
        where[longest] = (where[longest] + shift) % entries.shape[longest]
        spots.append(tuple(where))
    return entries.at[spots[0]].set(smallest).at[spots[1]].set(high)


def steps_of(own_key, dims, pieces, low, largest):
    gain = 1.0
    for position, blocks in pieces:
        draws = jax.random.uniform(jax.random.fold_in(jax.random.fold_in(own_key, 6), position), (blocks,), jnp.float32, low / len(pieces), largest / len(pieces))
        gain = gain * jnp.repeat(jnp.exp(draws), dims[position] // blocks).reshape((-1,) + (1,) * (len(dims) - 1 - position))
    return gain


def deal_out(rng, own, number, rows, number_of, top, bound, lean):
    order = jax.random.permutation(rng, number_of)
    packed, common = load_shares(number_of, rows * top, bound, lean, True), load_shares(number_of, rows * top, bound, lean, False)
    places = jnp.arange(number_of)

    def named(lengths, turn):
        used = int((lengths > 0).sum())
        fixed = max(1, used // 4)
        passed = fixed + (places - fixed + turn * (used - fixed)) % max(1, number_of - fixed)
        return jnp.zeros((number_of,), jnp.int32).at[order[jnp.where(places < fixed, places, passed)]].set(jnp.asarray(lengths, jnp.int32))

    lengths = jnp.where(number % 4 == 0, named(packed, number // 4), named(common, number - number // 4 - 1))
    mixed = jax.random.permutation(jax.random.fold_in(own, 3), number_of)
    giver, taker = mixed[0:number_of // 2 * 2:2], mixed[1:number_of // 2 * 2:2]
    margin = jnp.minimum(lengths[giver] - 1, bound - lengths[taker]) // 2
    margin = jnp.where((giver == order[0]) | (taker == order[0]) | (lengths[taker] == 0), 0, jnp.maximum(margin, 0))
    passed = jax.random.randint(jax.random.fold_in(own, 4), (number_of // 2,), 0, 1 << 20) % (margin + 1)
    lengths = lengths.at[giver].add(-passed).at[taker].add(passed)
    items = jnp.searchsorted(jnp.cumsum(lengths), jnp.arange(rows * top), side="right").astype(jnp.int32)
    listing = items.reshape(top, rows).T
    listing = listing[jax.random.permutation(jax.random.fold_in(own, 1), rows)]
    turn = jax.random.randint(jax.random.fold_in(own, 2), (rows, 1), 0, top)
    return jnp.take_along_axis(listing, (jnp.arange(top)[None, :] + turn) % top, axis=1)


def load_shares(amount, total, most, slope, full):
    weights = [(1 << 20) // math.isqrt(grade ** slope) + 1 for grade in range(1, amount + 1)]
    largest = most if full else min(most, max(-(-total // amount), total * weights[0] // sum(weights)))
    least = 1 if total - largest >= amount - 1 else 0
    counts, surplus = [largest] + [least] * (amount - 1), total - largest - least * (amount - 1)
    while surplus > 0:
        candidates = [i for i in range(1, amount) if counts[i] < largest] or [i for i in range(1, amount) if counts[i] < most]
        whole, remaining = sum([weights[i] for i in candidates]), surplus
        for i in candidates:
            more = min(most - counts[i], max(1, remaining * weights[i] // whole), surplus)
            counts[i] = counts[i] + more
            surplus = surplus - more
    return np.array(counts)


def gaussian(rng, shape, scale, reach, shards=(), kind=jnp.bfloat16):
    loudness = steps_of(rng, shape, shards, -0.22, 0.18) if shards else 1.0
    result = jax.random.normal(rng, shape, jnp.float32) * scale * loudness
    return jnp.minimum(jnp.maximum(result, -reach), reach).astype(kind)


def setup_inputs(seed: int = 0) -> dict:
    arg_keys = jax.random.split(jax.random.key(seed), 8)
    attention_output = gaussian(arg_keys[0], (TOKENS, MODEL_WIDTH), 1.0, 6.0, ((0, 8), (1, 32)))
    quantized_weight_codes = draw_quantized_weight_codes(jax.random.fold_in(arg_keys[7], 71), 0)
    column_scale = draw_column_scale(jax.random.fold_in(arg_keys[7], 71), 0)
    adapter_down_maps = gaussian(arg_keys[3], (ADAPTER_COUNT, ADAPTER_RANK, MODEL_WIDTH), MODEL_WIDTH ** -0.5, 0.0625, ((0, 8), (2, 32)))
    adapter_up_maps = gaussian(arg_keys[4], (ADAPTER_COUNT, ADAPTER_RANK, MODEL_WIDTH), ADAPTER_RANK ** -0.5, 0.75, ((0, 8), (2, 32)))
    owning_group_index_keys = jax.random.split(jax.random.fold_in(arg_keys[5], 1), TOKENS // TOK_GRP)
    owning_group_index_turns = jax.random.permutation(jax.random.fold_in(arg_keys[5], 3), TOKENS // TOK_GRP)
    owning_group_index = jax.vmap(lambda own, number: deal_out(jax.random.fold_in(arg_keys[5], 2), own, number, TOK_GRP, N_GRP, 1, CAP, 2))(owning_group_index_keys, owning_group_index_turns).reshape((TOKENS, 1))
    token_adapter_slot = plant(jax.random.randint(arg_keys[6], (TOKENS,), 0, ADAPT_GRP), jax.random.fold_in(arg_keys[6], 1), 0, ADAPT_GRP - 1).astype(jnp.int32)
    return dict(attention_output=attention_output, quantized_weight_codes=quantized_weight_codes, column_scale=column_scale, adapter_down_maps=adapter_down_maps, adapter_up_maps=adapter_up_maps, owning_group_index=owning_group_index, token_adapter_slot=token_adapter_slot)


def reference(attention_output, quantized_weight_codes, column_scale, adapter_down_maps, adapter_up_maps, owning_group_index, token_adapter_slot):
    summed = jnp.dot(attention_output, quantized_weight_codes, preferred_element_type=jnp.float32)
    base = summed * column_scale[None, :]
    adapter = (owning_group_index[:, 0] * ADAPT_GRP + token_adapter_slot).astype(jnp.int32)

    def one_token(token_pair):
        single_token_row, selected_adapter = token_pair
        rank_product = jnp.dot(adapter_down_maps[selected_adapter], single_token_row, preferred_element_type=jnp.float32).astype(jnp.bfloat16)
        return jnp.dot(rank_product, adapter_up_maps[selected_adapter], preferred_element_type=jnp.float32).astype(jnp.bfloat16)

    adapter_update = lax.map(one_token, (attention_output, adapter))
    adapter_update = lax.optimization_barrier(adapter_update)
    return (base + adapter_update.astype(jnp.float32)).astype(jnp.bfloat16)
```

```python
import jax
import jax.numpy as jnp
from jax import lax
from jax.experimental import pallas as pl
from jax.experimental.pallas import tpu as pltpu
from jax.sharding import Mesh, PartitionSpec as P

NX, NC, NY, NZ = 4, 2, 4, 8
GROUPS = NX * NC
CAP = 128
EXTRA = 16
ROWS = CAP + EXTRA
RANK = 64
F32, BF16 = jnp.float32, jnp.bfloat16
NT = (((1,), (1,)), ((), ()))


def params(mib=40):
    return pltpu.CompilerParams(vmem_limit_bytes=mib * 1024 * 1024)


def cost(flops, nbytes):
    return pl.CostEstimate(flops=flops, bytes_accessed=nbytes, transcendentals=0)


def pick_body(index_ref, w_ref, o_ref):
    o_ref[...] = w_ref[...]


def pick_block(weights, column, width):
    depth = weights.shape[0]
    return pl.pallas_call(
        pick_body,
        out_shape=jax.ShapeDtypeStruct((depth, NY * width), weights.dtype),
        grid_spec=pltpu.PrefetchScalarGridSpec(
            num_scalar_prefetch=1,
            grid=(NY,),
            in_specs=[pl.BlockSpec((depth, width), lambda i, at: (0, i * NZ + at[0]))],
            out_specs=pl.BlockSpec((depth, width), lambda i, at: (0, i)),
        ),
        compiler_params=params(),
        cost_estimate=cost(0, 4 * depth * NY * width),
    )(column, weights)


def route_body(owner_ref, slot_ref, rows_ref, send_ref, place_ref):
    tokens = rows_ref.shape[0]
    owner = owner_ref[...]
    member = lax.broadcasted_iota(jnp.int32, (GROUPS, tokens), 0) == owner
    before = lax.broadcasted_iota(jnp.int32, (tokens, tokens), 0) < lax.broadcasted_iota(
        jnp.int32, (tokens, tokens), 1
    )
    earlier = jnp.dot(
        member.astype(F32).astype(BF16), before.astype(F32).astype(BF16), preferred_element_type=F32
    )
    position = jnp.sum(jnp.where(member, earlier, 0.0), axis=0, keepdims=True)
    target = owner.astype(F32) * CAP + position
    rows = rows_ref[...]
    slots = jnp.broadcast_to(slot_ref[...].astype(F32), (EXTRA, tokens)).astype(BF16)
    for g in range(GROUPS):
        spot = lax.broadcasted_iota(jnp.int32, (CAP, tokens), 0).astype(F32) + float(g * CAP)
        select = jnp.where(spot == target, 1.0, 0.0).astype(BF16)
        send_ref[g, :CAP, :] = jnp.dot(select, rows, preferred_element_type=F32).astype(BF16)
        sent = lax.dot_general(slots, select, NT, preferred_element_type=F32).astype(BF16)
        send_ref[g, CAP:, :CAP] = sent
        send_ref[g, CAP:, CAP:] = sent
    same = lax.broadcasted_iota(jnp.int32, (tokens, tokens), 0) == lax.broadcasted_iota(
        jnp.int32, (tokens, tokens), 1
    )
    column = jnp.sum(jnp.where(same, target, 0.0), axis=1, keepdims=True)
    place_ref[...] = jnp.broadcast_to(column, place_ref.shape)


def route(owner, slot, rows):
    tokens, width = rows.shape
    return pl.pallas_call(
        route_body,
        out_shape=(
            jax.ShapeDtypeStruct((GROUPS, ROWS, width), BF16),
            jax.ShapeDtypeStruct((tokens, 128), F32),
        ),
        compiler_params=params(),
        cost_estimate=cost(2 * GROUPS * CAP * tokens * width, 4 * GROUPS * ROWS * width),
    )(owner, slot, rows)


def down_body(got_ref, map_ref, low_ref, diff_ref, rows_ref, total_ref):
    step = pl.program_id(0)
    half = lax.broadcasted_iota(jnp.int32, (CAP, 128), 1) >= RANK

    @pl.when(step == 0)
    def _():
        same = lax.broadcasted_iota(jnp.int32, (CAP, CAP), 0) == lax.broadcasted_iota(
            jnp.int32, (CAP, CAP), 1
        )
        ones = jnp.ones((CAP, 128), BF16)
        for g in range(GROUPS):
            rows_ref[g * CAP : (g + 1) * CAP, :] = got_ref[g, :CAP, :]
            slot = got_ref[g, CAP:, :CAP].astype(F32)[:1, :]
            spread = jnp.where(same, slot, 0.0).astype(BF16)
            slots = jnp.dot(spread, ones, preferred_element_type=F32)
            diff_ref[g * CAP : (g + 1) * CAP, :] = slots - jnp.where(half, 1.0, 0.0)
        total_ref[...] = jnp.zeros_like(total_ref)

    wide = map_ref.shape[0]
    for n in range(wide // 256):
        product = lax.dot_general(
            rows_ref[...], map_ref[n * 256 : (n + 1) * 256, :], NT, preferred_element_type=F32
        )
        base = (step * (wide // RANK) + n * 4).astype(F32)
        total_ref[...] += jnp.where(diff_ref[...] == base, product[:, :128], 0.0) + jnp.where(
            diff_ref[...] == base + 2.0, product[:, 128:], 0.0
        )

    @pl.when(step == pl.num_programs(0) - 1)
    def _():
        whole = total_ref[...]
        whole = whole + pltpu.roll(whole, RANK, 1)
        packed = whole.shape[0] // 2
        left = lax.broadcasted_iota(jnp.int32, (packed, 128), 1) < RANK
        low_ref[...] = jnp.where(left, whole[:packed], whole[packed:])


def down(got, maps, steps=8):
    wide, width = maps.shape
    rows = GROUPS * CAP
    return pl.pallas_call(
        down_body,
        out_shape=(
            jax.ShapeDtypeStruct((rows // 2, 128), F32),
            jax.ShapeDtypeStruct((rows, 128), F32),
        ),
        grid=(steps,),
        in_specs=[
            pl.BlockSpec(got.shape, lambda i: (0, 0, 0)),
            pl.BlockSpec((wide // steps, width), lambda i: (i, 0)),
        ],
        out_specs=(
            pl.BlockSpec((rows // 2, 128), lambda i: (0, 0)),
            pl.BlockSpec((rows, 128), lambda i: (0, 0)),
        ),
        scratch_shapes=[pltpu.VMEM((rows, width), BF16), pltpu.VMEM((rows, 128), F32)],
        compiler_params=params(),
        cost_estimate=cost(2 * rows * wide * width, 2 * wide * width),
    )(got, maps)


def total_body(parts_ref, o_ref):
    whole = jnp.sum(parts_ref[...], axis=0).astype(BF16)
    o_ref[...] = jnp.broadcast_to(whole[None], o_ref.shape)


def total(parts):
    return pl.pallas_call(
        total_body,
        out_shape=jax.ShapeDtypeStruct(parts.shape, BF16),
        compiler_params=params(),
        cost_estimate=cost(parts.size, 6 * parts.size),
    )(parts)


def up_body(low_ref, diff_ref, map_ref, o_ref, twice_ref, total_ref):
    step = pl.program_id(0)

    @pl.when(step == 0)
    def _():
        packed = low_ref[...].astype(F32)
        swapped = pltpu.roll(packed, RANK, 1)
        left = lax.broadcasted_iota(jnp.int32, packed.shape, 1) < RANK
        twice_ref[: packed.shape[0], :] = jnp.where(left, packed, swapped)
        twice_ref[packed.shape[0] :, :] = jnp.where(left, swapped, packed)
        total_ref[...] = jnp.zeros_like(total_ref)

    wide = map_ref.shape[0]
    diff, twice = diff_ref[...], twice_ref[...]
    pieces = []
    for n in range(wide // 128):
        base = (step * (wide // RANK) + n * 2).astype(F32)
        pieces.append(jnp.where(diff == base, twice, 0.0).astype(BF16))
    total_ref[...] += jnp.dot(
        jnp.concatenate(pieces, axis=1), map_ref[...], preferred_element_type=F32
    )

    @pl.when(step == pl.num_programs(0) - 1)
    def _():
        o_ref[...] = total_ref[...].astype(BF16).reshape(o_ref.shape)


def up(low, diff, maps, steps=8):
    wide, width = maps.shape
    rows = GROUPS * CAP
    return pl.pallas_call(
        up_body,
        out_shape=jax.ShapeDtypeStruct((GROUPS, CAP, width), BF16),
        grid=(steps,),
        in_specs=[
            pl.BlockSpec(low.shape, lambda i: (0, 0)),
            pl.BlockSpec(diff.shape, lambda i: (0, 0)),
            pl.BlockSpec((wide // steps, width), lambda i: (i, 0)),
        ],
        out_specs=pl.BlockSpec((GROUPS, CAP, width), lambda i: (0, 0, 0)),
        scratch_shapes=[pltpu.VMEM((rows, 128), F32), pltpu.VMEM((rows, width), F32)],
        compiler_params=params(),
        cost_estimate=cost(2 * rows * wide * width, 2 * wide * width),
    )(low, diff, maps)


def base_body(index_ref, a_ref, *refs):
    o_ref = refs[-1]
    whole = jnp.zeros(o_ref.shape[1:], F32)
    for core in range(NC):
        own, left, right, top, bottom = refs[5 * core : 5 * core + 5]
        far = jnp.concatenate([top[...], bottom[...]], axis=0)
        for at, block in enumerate((own[...], left[...], right[...], far)):
            whole += jnp.dot(
                a_ref[index_ref[4 * core + at]], block, preferred_element_type=F32
            )
    o_ref[0] = whole.astype(BF16)


def base_product(index, gathered, pieces, width):
    depth = gathered.shape[2]
    tokens = gathered.shape[1]
    specs = [
        pl.BlockSpec((piece.shape[0], width), lambda i, at: (0, i)) for piece in pieces
    ]
    return pl.pallas_call(
        base_body,
        out_shape=jax.ShapeDtypeStruct((NY, tokens, width), BF16),
        grid_spec=pltpu.PrefetchScalarGridSpec(
            num_scalar_prefetch=1,
            grid=(NY,),
            in_specs=[pl.BlockSpec(gathered.shape, lambda i, at: (0, 0, 0))] + specs,
            out_specs=pl.BlockSpec((1, tokens, width), lambda i, at: (i, 0, 0)),
        ),
        compiler_params=params(),
        cost_estimate=cost(2 * tokens * NZ * depth * NY * width, 8 * 1024 * 1024),
    )(index, gathered, *pieces)


def final_body(parts_ref, scale_ref, place_ref, back_ref, o_ref):
    summed = jnp.sum(parts_ref[...].astype(F32), axis=0)
    place = place_ref[...]
    lane = lax.broadcasted_iota(jnp.int32, place.shape, 1).astype(F32)
    pieces = [
        jnp.where(place == lane + float(g * CAP), 1.0, 0.0).astype(BF16) for g in range(GROUPS)
    ]
    delta = jnp.dot(
        jnp.concatenate(pieces, axis=1),
        back_ref[...].reshape(GROUPS * CAP, back_ref.shape[2]),
        preferred_element_type=F32,
    )
    o_ref[...] = (summed * scale_ref[...] + delta).astype(BF16)


def final(parts, scale, place, back):
    return pl.pallas_call(
        final_body,
        out_shape=jax.ShapeDtypeStruct(parts.shape[1:], BF16),
        compiler_params=params(),
        cost_estimate=cost(2 * GROUPS * CAP * parts.shape[1] * parts.shape[2], 4 * 1024 * 1024),
    )(parts, scale, place, back)


def shift(a, axis, by, size):
    return lax.ppermute(a, axis, [(i, (i + by) % size) for i in range(size)])


def on_device(rows, weights, scale, down_maps, up_maps, owner, slot):
    tokens, width = rows.shape
    x, c, z = lax.axis_index("x"), lax.axis_index("c"), lax.axis_index("z")

    turn = x + NX * c
    picked = pick_block(weights, ((z + turn) % NZ).reshape(1), width)
    pairs = []
    for at in range(NX * NC * NZ):
        i, j, k = at // (NC * NZ), at // NZ % NC, at % NZ
        pairs.append((at, (i * NC + j) * NZ + (k + i + NX * j) % NZ))
    own = lax.ppermute(picked, ("x", "c", "z"), pairs)
    gathered = lax.all_gather(rows, "z")

    send, place = route(owner.reshape(1, tokens), slot.reshape(1, tokens), rows)
    got = lax.all_to_all(send, ("x", "c"), 0, 0, tiled=True)

    left = shift(own, "x", 1, NX)
    right = shift(own, "x", -1, NX)
    depth = own.shape[0] // 2
    top = shift(left[:depth], "x", 1, NX)
    bottom = shift(right[depth:], "x", -1, NX)
    mine = [own, left, right, top, bottom]
    other = [shift(piece, "c", 1, NC) for piece in mine]

    low_part, diff = down(got, down_maps.reshape(-1, width))
    low_part = low_part.reshape(NY * NZ, -1, 128)
    low_all = total(lax.all_to_all(low_part, ("y", "z"), 0, 0, tiled=True))
    low = lax.all_to_all(low_all, ("y", "z"), 0, 0, tiled=True).reshape(-1, 128)
    delta = up(low, diff, up_maps.reshape(-1, width))
    back = lax.all_to_all(delta, ("x", "c"), 0, 0, tiled=True)

    turns = [x, x - 1, x + 1, x + 2]
    index = jnp.stack(
        [(z - (t % NX) - NX * k) % NZ for k in (c, 1 - c) for t in turns]
    ).astype(jnp.int32)
    parts = base_product(index, gathered, mine + other, width)
    parts = lax.all_to_all(parts, "y", 0, 0, tiled=True)
    return final(parts, scale.reshape(1, width), place, back)


def solution(mesh):
    fine = Mesh(mesh.devices.reshape(NX, NC, NY, NZ), ("x", "c", "y", "z"))
    grp, tp = ("x", "c"), ("y", "z")
    in_specs = (
        P(grp, tp),
        P(tp, None),
        P(tp),
        P(grp, None, tp),
        P(grp, None, tp),
        P(grp, None),
        P(grp),
    )
    return jax.shard_map(
        on_device, mesh=fine, in_specs=in_specs, out_specs=P(grp, tp), check_vma=False
    )
```

```python
import jax
import jax.numpy as jnp
from jax import lax
from jax.experimental import pallas as pl
from jax.experimental.pallas import tpu as pltpu
from jax.sharding import Mesh, PartitionSpec as P

NX, NC, NY, NZ = 4, 2, 4, 8
GROUPS = NX * NC
CAP = 128
EXTRA = 16
ROWS = CAP + EXTRA
RANK = 64
PARTS = 2
F32, BF16 = jnp.float32, jnp.bfloat16
NT = (((1,), (1,)), ((), ()))
TN = (((0,), (0,)), ((), ()))
LOCAL = pl.BlockSpec(memory_space=pltpu.VMEM)
REMOTE = pl.BlockSpec(memory_space=pltpu.HBM)
ANY = pl.BlockSpec(memory_space=pl.ANY)


def in_hbm(a):
    return pltpu.with_memory_space_constraint(a, pltpu.HBM)


def params(mib=12):
    return pltpu.CompilerParams(vmem_limit_bytes=mib * 1024 * 1024)


def cost(flops, nbytes):
    return pl.CostEstimate(flops=8 * flops, bytes_accessed=8 * nbytes, transcendentals=0)


def turn_of(chunk, x, c):
    return (x if chunk == 0 else x + 1 - 2 * (x % 2)) + NX * c


CHUNKS = ((2, 1), (3, 0))


def start_body(
    owner_ref, slot_ref, rows_ref, w_ref, first_ref, second_ref, send_ref, target_ref, sem
):
    x, c, y, z = (lax.axis_index(name) for name in ("x", "c", "y", "z"))
    width = rows_ref.shape[1]
    copies = []
    for chunk, out in enumerate((first_ref, second_ref)):
        column = (z + turn_of(chunk, x, c)) % NZ
        for at, by in enumerate(CHUNKS[chunk]):
            offset = pl.multiple_of(((y + by) % NY * NZ + column) * width, 256)
            copies.append(
                pltpu.make_async_copy(
                    w_ref.at[:, pl.ds(offset, width)],
                    out.at[:, pl.ds(at * width, width)],
                    sem.at[2 * chunk + at],
                )
            )
    for copy in copies:
        copy.start()

    tokens = rows_ref.shape[0]
    owner = owner_ref[...]
    member = lax.broadcasted_iota(jnp.int32, (GROUPS, tokens), 0) == owner
    before = lax.broadcasted_iota(jnp.int32, (tokens, tokens), 0) < lax.broadcasted_iota(
        jnp.int32, (tokens, tokens), 1
    )
    earlier = jnp.dot(
        member.astype(F32).astype(BF16), before.astype(F32).astype(BF16), preferred_element_type=F32
    )
    position = jnp.sum(jnp.where(member, earlier, 0.0), axis=0, keepdims=True)
    target = owner.astype(F32) * CAP + position
    target_ref[...] = jnp.broadcast_to(target, target_ref.shape)
    rows = rows_ref[...]
    slots = jnp.broadcast_to(slot_ref[...].astype(F32), (EXTRA, tokens)).astype(BF16)
    for g in range(GROUPS):
        spot = lax.broadcasted_iota(jnp.int32, (CAP, tokens), 0).astype(F32) + float(g * CAP)
        select = jnp.where(spot == target, 1.0, 0.0).astype(BF16)
        send_ref[g, :CAP, :] = jnp.dot(select, rows, preferred_element_type=F32).astype(BF16)
        sent = lax.dot_general(slots, select, NT, preferred_element_type=F32).astype(BF16)
        send_ref[g, CAP:, :CAP] = sent
        send_ref[g, CAP:, CAP:] = sent
    for copy in copies:
        copy.wait()


def start(owner, slot, rows, weights):
    tokens, width = rows.shape
    depth = weights.shape[0]
    return pl.pallas_call(
        start_body,
        out_shape=(
            pltpu.VMEM((depth, 2 * width), BF16),
            pltpu.VMEM((depth, 2 * width), BF16),
            pltpu.HBM((GROUPS, ROWS, width), BF16),
            jax.ShapeDtypeStruct((8, tokens), F32),
        ),
        in_specs=[LOCAL, LOCAL, LOCAL, REMOTE],
        out_specs=(LOCAL, LOCAL, LOCAL, LOCAL),
        scratch_shapes=[pltpu.SemaphoreType.DMA((4,))],
        compiler_params=params(),
        cost_estimate=cost(2 * GROUPS * CAP * tokens * width, 4 * GROUPS * ROWS * width),
    )(in_hbm(owner), in_hbm(slot), in_hbm(rows), in_hbm(weights))


def fetch(source, target, sem, parts):
    size = source.shape[0] // parts
    copies = []
    for i in range(parts):
        here = pl.ds(i * size, size)
        copies.append(pltpu.make_async_copy(source.at[here], target.at[here], sem.at[i]))
    for copy in copies:
        copy.start()
    return copies


def down_body(got_ref, source_ref, *refs):
    low_ref, slot_ref, map_ref, total_ref, sem = refs[-5:]
    copies = fetch(source_ref, map_ref, sem, PARTS)
    slot = jnp.concatenate(
        [got_ref[g, CAP:, :CAP].astype(F32)[:1, :] for g in range(GROUPS)], axis=1
    )
    slot_ref[...] = jnp.broadcast_to(slot, slot_ref.shape)
    per = map_ref.shape[0] // PARTS // 256
    for p in range(PARTS):
        copies[p].wait()
        for b in range(GROUPS // 2):
            rows = jnp.concatenate([got_ref[2 * b, :CAP, :], got_ref[2 * b + 1, :CAP, :]], axis=0)
            columns = slice(2 * b * CAP, 2 * (b + 1) * CAP)
            here = slot[:, columns]
            total = total_ref[:, columns] if p else jnp.zeros((RANK, 2 * CAP), F32)
            for n in range(p * per, (p + 1) * per):
                product = lax.dot_general(
                    map_ref[n * 256 : (n + 1) * 256, :], rows, NT, preferred_element_type=F32
                )
                for j in range(256 // RANK):
                    part = product[RANK * j : RANK * (j + 1), :]
                    total = jnp.where(here == float(n * 256 // RANK + j), part, total)
            if p < PARTS - 1:
                total_ref[:, columns] = total
                continue
            for g in range(2):
                for i in range(RANK // 16):
                    low_ref[(2 * b + g) * (RANK // 16) + i] = total[
                        16 * i : 16 * (i + 1), g * CAP : (g + 1) * CAP
                    ]


def down(got, maps, *deps):
    rows, width = GROUPS * CAP, maps.shape[1]
    return pl.pallas_call(
        down_body,
        out_shape=(
            pltpu.HBM((NY * NZ, 16, CAP), F32),
            jax.ShapeDtypeStruct((8, rows), F32),
        ),
        in_specs=[LOCAL, REMOTE] + [ANY] * len(deps),
        out_specs=(LOCAL, LOCAL),
        scratch_shapes=[
            pltpu.VMEM(maps.shape, BF16),
            pltpu.VMEM((RANK, rows), F32),
            pltpu.SemaphoreType.DMA((PARTS,)),
        ],
        compiler_params=params(),
        cost_estimate=cost(2 * rows * maps.shape[0] * width, 2 * maps.shape[0] * width),
    )(got, in_hbm(maps), *deps)


def total_body(parts_ref, *refs):
    o_ref = refs[-1]
    whole = jnp.sum(parts_ref[...], axis=0).astype(BF16)
    o_ref[...] = jnp.broadcast_to(whole[None], o_ref.shape)


def total(parts, *deps):
    return pl.pallas_call(
        total_body,
        out_shape=pltpu.HBM(parts.shape, BF16),
        in_specs=[LOCAL] + [ANY] * len(deps),
        out_specs=LOCAL,
        compiler_params=params(4),
        cost_estimate=cost(parts.size, 6 * parts.size),
    )(parts, *deps)


def up_body(low_ref, slot_ref, source_ref, *refs):
    o_ref, token_ref, map_ref, sem = refs[-4:]
    token_ref[...] = slot_ref[:, :128]
    copies = fetch(source_ref, map_ref, sem, PARTS)
    per = RANK // 16
    for b in range(GROUPS // 2):
        halves = [
            jnp.concatenate([low_ref[g * per + i].astype(F32) for i in range(per)], axis=0)
            for g in (2 * b, 2 * b + 1)
        ]
        low = jnp.concatenate(halves, axis=1)
        here = slot_ref[:1, 2 * b * CAP : 2 * (b + 1) * CAP]
        spread = jnp.concatenate(
            [
                jnp.where(here == float(a), low, 0.0).astype(BF16)
                for a in range(map_ref.shape[0] // RANK)
            ],
            axis=0,
        )
        if b == 0:
            for copy in copies:
                copy.wait()
        out = lax.dot_general(spread, map_ref[...], TN, preferred_element_type=F32).astype(BF16)
        o_ref[2 * b] = out[:CAP]
        o_ref[2 * b + 1] = out[CAP:]


def up(low, slots, maps, *deps):
    rows, width = GROUPS * CAP, maps.shape[1]
    return pl.pallas_call(
        up_body,
        out_shape=(
            pltpu.HBM((GROUPS, CAP, width), BF16),
            jax.ShapeDtypeStruct((8, 128), F32),
        ),
        in_specs=[LOCAL, LOCAL, REMOTE] + [ANY] * len(deps),
        out_specs=(LOCAL, LOCAL),
        scratch_shapes=[pltpu.VMEM(maps.shape, BF16), pltpu.SemaphoreType.DMA((PARTS,))],
        compiler_params=params(20),
        cost_estimate=cost(2 * rows * maps.shape[0] * width, 2 * maps.shape[0] * width),
    )(low, slots, in_hbm(maps), *deps)


def base_body(chunk, *refs):
    ring, pieces = refs[:NZ], refs[NZ : 2 * NZ]
    o_ref, p_ref, token_ref, a_ref, w_ref, sem = refs[-6:]
    token_ref[...] = jnp.zeros_like(token_ref)
    x, c = lax.axis_index("x"), lax.axis_index("c")
    depth, width = w_ref.shape[1], o_ref.shape[1]
    copies = []
    for at, slot in enumerate((0, 1, 7, 2, 6, 3, 5, 4)):
        copies.append(pltpu.make_async_copy(ring[at], a_ref.at[slot], sem.at[at]))
    turns = [x, x + NX - 1, x + 1, x + 2]
    for at in range(NZ):
        slot = turn_of(chunk, turns[at % NX] % NX, c if at < NX else 1 - c)
        copies.append(pltpu.make_async_copy(pieces[at], w_ref.at[slot], sem.at[NZ + at]))
    for copy in copies:
        copy.start()
    for copy in copies:
        copy.wait()
    whole = jnp.dot(
        jnp.concatenate([a_ref[k] for k in range(NZ)], axis=1),
        w_ref[...].reshape(NZ * depth, w_ref.shape[2]),
        preferred_element_type=F32,
    )
    o_ref[...] = whole[:, :width].astype(BF16)
    p_ref[...] = whole[:, width:].astype(BF16)


def base_product(chunk, ring, pieces, space, *deps):
    tokens, width = ring[0].shape
    depth, wide = pieces[0].shape

    def body(*refs):
        base_body(chunk, *refs)

    return pl.pallas_call(
        body,
        out_shape=[space((tokens, width), BF16)] * 2 + [jax.ShapeDtypeStruct((8, 128), F32)],
        in_specs=[ANY] * (2 * NZ + len(deps)),
        out_specs=[LOCAL] * 3,
        scratch_shapes=[
            pltpu.VMEM((NZ, tokens, width), BF16),
            pltpu.VMEM((NZ, depth, wide), BF16),
            pltpu.SemaphoreType.DMA((2 * NZ,)),
        ],
        compiler_params=params(),
        cost_estimate=cost(2 * tokens * NZ * depth * wide, 4 * 1024 * 1024),
    )(*ring, *pieces, *deps)


def final_body(*refs):
    parts, (scale_ref, target_ref, back_ref, o_ref) = refs[:NY], refs[NY:]
    tokens = o_ref.shape[0]
    back = back_ref[...].reshape(GROUPS * CAP, back_ref.shape[2])
    step = 256
    for b in range(tokens // step):
        here = slice(b * step, (b + 1) * step)
        spot = lax.broadcasted_iota(jnp.int32, (GROUPS * CAP, step), 0).astype(F32)
        select = jnp.where(spot == target_ref[:1, here], 1.0, 0.0).astype(BF16)
        delta = lax.dot_general(select, back, TN, preferred_element_type=F32)
        summed = parts[0][here, :].astype(F32)
        for part in parts[1:]:
            summed += part[here, :].astype(F32)
        o_ref[here, :] = (summed * scale_ref[...] + delta).astype(BF16)


def final(parts, scale, target, back):
    tokens, width = parts[0].shape
    return pl.pallas_call(
        final_body,
        out_shape=jax.ShapeDtypeStruct((tokens, width), BF16),
        in_specs=[LOCAL] * (NY + 3),
        out_specs=LOCAL,
        compiler_params=params(),
        cost_estimate=cost(2 * GROUPS * CAP * tokens * width, 4 * 1024 * 1024),
    )(*parts, scale, target, back)


def shift(a, axis, by, size):
    return lax.ppermute(a, axis, [(i, (i + by) % size) for i in range(size)])


def pass_on(chunk, a):
    pairs = []
    for at in range(NX * NC * NZ):
        i, j, k = at // (NC * NZ), at // NZ % NC, at % NZ
        pairs.append((at, (i * NC + j) * NZ + (k + turn_of(chunk, i, j)) % NZ))
    return lax.ppermute(a, ("x", "c", "z"), pairs)


def on_device(rows, weights, scale, down_maps, up_maps, owner, slot):
    tokens, width = rows.shape
    first, second, send, target = start(
        owner.reshape(1, tokens), slot.reshape(1, tokens), rows, weights
    )
    owns = [pass_on(0, first), pass_on(1, second)]
    got = lax.all_to_all(send, ("x", "c"), 0, 0, tiled=True)
    ring = [rows, shift(rows, "z", 1, NZ), shift(rows, "z", -1, NZ)]

    low_part, slots = down(got, down_maps.reshape(-1, width), *owns, *ring[1:])
    lefts = [shift(own, "x", 1, NX) for own in owns]
    rights = [shift(own, "x", -1, NX) for own in owns]
    ring += [shift(ring[1], "z", 1, NZ), shift(ring[2], "z", -1, NZ)]
    ring += [shift(ring[3], "z", 1, NZ), shift(ring[4], "z", -1, NZ)]

    low_part = lax.all_to_all(low_part, ("y", "z"), 0, 0, tiled=True)
    low_all = total(low_part, *lefts, *rights, *ring[3:])
    low = lax.all_to_all(low_all, ("y", "z"), 0, 0, tiled=True)

    ring.append(shift(ring[5], "z", 1, NZ))
    fars = [shift(lefts[0], "x", 1, NX), shift(rights[1], "x", -1, NX)]
    chunks = []
    for mine in zip(owns, lefts, rights, fars):
        chunks.append([*mine, *(shift(piece, "c", 1, NC) for piece in mine)])

    two, one, token = base_product(0, ring, chunks[0], pltpu.HBM)
    delta, token = up(low, slots, up_maps.reshape(-1, width), token)
    back = lax.all_to_all(delta, ("x", "c"), 0, 0, tiled=True)

    three, zero, _ = base_product(1, ring, chunks[1], pltpu.VMEM, token)
    parts = [zero, shift(one, "y", 1, NY), shift(two, "y", 2, NY), shift(three, "y", 3, NY)]
    return final(parts, scale.reshape(1, width), target, back)


def solution(mesh):
    fine = Mesh(mesh.devices.reshape(NX, NC, NY, NZ), ("x", "c", "y", "z"))
    grp, tp = ("x", "c"), ("y", "z")
    in_specs = (
        P(grp, tp),
        P(tp, None),
        P(tp),
        P(grp, None, tp),
        P(grp, None, tp),
        P(grp, None),
        P(grp),
    )
    return jax.shard_map(
        on_device, mesh=fine, in_specs=in_specs, out_specs=P(grp, tp), check_vma=False
    )
```

```python
import jax
import jax.numpy as jnp
from jax import lax
from jax.experimental import pallas as pl
from jax.experimental.pallas import tpu as pltpu
from jax.sharding import Mesh, PartitionSpec as P

NX, NC, NY, NZ = 4, 2, 4, 8
GROUPS = NX * NC
CAP = 128
EXTRA = 16
ROWS = CAP + EXTRA
RANK = 64
PARTS = 2
F32, BF16 = jnp.float32, jnp.bfloat16
NT = (((1,), (1,)), ((), ()))
TN = (((0,), (0,)), ((), ()))
LOCAL = pl.BlockSpec(memory_space=pltpu.VMEM)
REMOTE = pl.BlockSpec(memory_space=pltpu.HBM)
ANY = pl.BlockSpec(memory_space=pl.ANY)


def in_hbm(a):
    return pltpu.with_memory_space_constraint(a, pltpu.HBM)


def params(mib=12):
    return pltpu.CompilerParams(vmem_limit_bytes=mib * 1024 * 1024)


def cost(flops, nbytes):
    return pl.CostEstimate(flops=flops, bytes_accessed=nbytes, transcendentals=0)


def turn_of(chunk, x, c):
    return (x if chunk == 0 else x + 1 - 2 * (x % 2)) + NX * c


WEIGHT = (4, 4)
CHUNKS = ((2, 1), (3, 0))


def start_body(
    owner_ref, slot_ref, rows_ref, w_ref, first_ref, second_ref, send_ref, target_ref, sem
):
    x, c, y, z = (lax.axis_index(name) for name in ("x", "c", "y", "z"))
    width = rows_ref.shape[1]
    copies = []
    for chunk, out in enumerate((first_ref, second_ref)):
        column = (z + turn_of(chunk, x, c)) % NZ
        for at, by in enumerate(CHUNKS[chunk]):
            offset = pl.multiple_of(((y + by) % NY * NZ + column) * width, 256)
            copies.append(
                pltpu.make_async_copy(
                    w_ref.at[:, pl.ds(offset, width)],
                    out.at[:, pl.ds(at * width, width)],
                    sem.at[2 * chunk + at],
                )
            )
    for copy in copies:
        copy.start()

    tokens = rows_ref.shape[0]
    owner = owner_ref[...]
    member = lax.broadcasted_iota(jnp.int32, (GROUPS, tokens), 0) == owner
    before = lax.broadcasted_iota(jnp.int32, (tokens, tokens), 0) < lax.broadcasted_iota(
        jnp.int32, (tokens, tokens), 1
    )
    earlier = jnp.dot(
        member.astype(F32).astype(BF16), before.astype(F32).astype(BF16), preferred_element_type=F32
    )
    position = jnp.sum(jnp.where(member, earlier, 0.0), axis=0, keepdims=True)
    target = owner.astype(F32) * CAP + position
    target_ref[...] = jnp.broadcast_to(target, target_ref.shape)
    rows = rows_ref[...]
    slots = jnp.broadcast_to(slot_ref[...].astype(F32), (EXTRA, tokens)).astype(BF16)
    for g in range(GROUPS):
        spot = lax.broadcasted_iota(jnp.int32, (CAP, tokens), 0).astype(F32) + float(g * CAP)
        select = jnp.where(spot == target, 1.0, 0.0).astype(BF16)
        send_ref[g, :CAP, :] = jnp.dot(select, rows, preferred_element_type=F32).astype(BF16)
        sent = lax.dot_general(slots, select, NT, preferred_element_type=F32).astype(BF16)
        send_ref[g, CAP:, :CAP] = sent
        send_ref[g, CAP:, CAP:] = sent
    for copy in copies:
        copy.wait()


def start(owner, slot, rows, weights):
    tokens, width = rows.shape
    depth = weights.shape[0]
    return pl.pallas_call(
        start_body,
        out_shape=(
            pltpu.VMEM((depth, 2 * width), BF16),
            pltpu.VMEM((depth, 2 * width), BF16),
            pltpu.HBM((GROUPS, ROWS, width), BF16),
            jax.ShapeDtypeStruct((8, tokens), F32),
        ),
        in_specs=[LOCAL, LOCAL, LOCAL, REMOTE],
        out_specs=(LOCAL, LOCAL, LOCAL, LOCAL),
        scratch_shapes=[pltpu.SemaphoreType.DMA((4,))],
        compiler_params=params(),
        cost_estimate=cost(8 * (2 * GROUPS * CAP * tokens * width), 8 * (4 * GROUPS * ROWS * width)),
    )(in_hbm(owner), in_hbm(slot), in_hbm(rows), in_hbm(weights))


def fetch(source, target, sem, parts):
    size = source.shape[0] // parts
    copies = []
    for i in range(parts):
        here = pl.ds(i * size, size)
        copies.append(pltpu.make_async_copy(source.at[here], target.at[here], sem.at[i]))
    for copy in copies:
        copy.start()
    return copies


def down_body(got_ref, source_ref, *refs):
    low_ref, slot_ref, map_ref, total_ref, sem = refs[-5:]
    copies = fetch(source_ref, map_ref, sem, PARTS)
    slot = jnp.concatenate(
        [got_ref[g, CAP:, :CAP].astype(F32)[:1, :] for g in range(GROUPS)], axis=1
    )
    slot_ref[...] = jnp.broadcast_to(slot, slot_ref.shape)
    per = map_ref.shape[0] // PARTS // 256
    for p in range(PARTS):
        copies[p].wait()
        for b in range(GROUPS // 2):
            rows = jnp.concatenate([got_ref[2 * b, :CAP, :], got_ref[2 * b + 1, :CAP, :]], axis=0)
            columns = slice(2 * b * CAP, 2 * (b + 1) * CAP)
            here = slot[:, columns]
            total = total_ref[:, columns] if p else jnp.zeros((RANK, 2 * CAP), F32)
            for n in range(p * per, (p + 1) * per):
                product = lax.dot_general(
                    map_ref[n * 256 : (n + 1) * 256, :], rows, NT, preferred_element_type=F32
                )
                for j in range(256 // RANK):
                    part = product[RANK * j : RANK * (j + 1), :]
                    total = jnp.where(here == float(n * 256 // RANK + j), part, total)
            if p < PARTS - 1:
                total_ref[:, columns] = total
                continue
            for g in range(2):
                for i in range(RANK // 16):
                    low_ref[(2 * b + g) * (RANK // 16) + i] = total[
                        16 * i : 16 * (i + 1), g * CAP : (g + 1) * CAP
                    ]


def down(got, maps, *deps):
    rows, width = GROUPS * CAP, maps.shape[1]
    return pl.pallas_call(
        down_body,
        out_shape=(
            pltpu.HBM((NY * NZ, 16, CAP), F32),
            jax.ShapeDtypeStruct((8, rows), F32),
        ),
        in_specs=[LOCAL, REMOTE] + [ANY] * len(deps),
        out_specs=(LOCAL, LOCAL),
        scratch_shapes=[
            pltpu.VMEM(maps.shape, BF16),
            pltpu.VMEM((RANK, rows), F32),
            pltpu.SemaphoreType.DMA((PARTS,)),
        ],
        compiler_params=params(),
        cost_estimate=cost(30 * (2 * rows * maps.shape[0] * width), 30 * (2 * maps.shape[0] * width)),
    )(got, in_hbm(maps), *deps)


def total_body(parts_ref, *refs):
    o_ref, token_ref = refs[-2:]
    token_ref[...] = parts_ref[0, :8, :]
    whole = jnp.sum(parts_ref[...], axis=0).astype(BF16)
    o_ref[...] = jnp.broadcast_to(whole[None], o_ref.shape)


def total(parts, *deps):
    return pl.pallas_call(
        total_body,
        out_shape=(pltpu.HBM(parts.shape, BF16), jax.ShapeDtypeStruct((8, 128), F32)),
        in_specs=[LOCAL] + [ANY] * len(deps),
        out_specs=(LOCAL, LOCAL),
        compiler_params=params(4),
        cost_estimate=cost(30 * (parts.size), 30 * (6 * parts.size)),
    )(parts, *deps)


def up_body(low_ref, slot_ref, source_ref, *refs):
    o_ref, token_ref, map_ref, sem = refs[-4:]
    token_ref[...] = slot_ref[:, :128]
    copies = fetch(source_ref, map_ref, sem, PARTS)
    per = RANK // 16
    for b in range(GROUPS // 2):
        halves = [
            jnp.concatenate([low_ref[g * per + i].astype(F32) for i in range(per)], axis=0)
            for g in (2 * b, 2 * b + 1)
        ]
        low = jnp.concatenate(halves, axis=1)
        here = slot_ref[:1, 2 * b * CAP : 2 * (b + 1) * CAP]
        spread = jnp.concatenate(
            [
                jnp.where(here == float(a), low, 0.0).astype(BF16)
                for a in range(map_ref.shape[0] // RANK)
            ],
            axis=0,
        )
        if b == 0:
            for copy in copies:
                copy.wait()
        out = lax.dot_general(spread, map_ref[...], TN, preferred_element_type=F32).astype(BF16)
        o_ref[2 * b] = out[:CAP]
        o_ref[2 * b + 1] = out[CAP:]


def up(low, slots, maps, *deps):
    rows, width = GROUPS * CAP, maps.shape[1]
    return pl.pallas_call(
        up_body,
        out_shape=(
            pltpu.HBM((GROUPS, CAP, width), BF16),
            jax.ShapeDtypeStruct((8, 128), F32),
        ),
        in_specs=[LOCAL, LOCAL, REMOTE] + [ANY] * len(deps),
        out_specs=(LOCAL, LOCAL),
        scratch_shapes=[pltpu.VMEM(maps.shape, BF16), pltpu.SemaphoreType.DMA((PARTS,))],
        compiler_params=params(20),
        cost_estimate=cost(30 * (2 * rows * maps.shape[0] * width), 30 * (2 * maps.shape[0] * width)),
    )(low, slots, in_hbm(maps), *deps)


def base_body(chunk, *refs):
    ring, pieces = refs[:NZ], refs[NZ : 2 * NZ]
    o_ref, p_ref, token_ref, a_ref, w_ref, sem = refs[-6:]
    token_ref[...] = jnp.zeros_like(token_ref)
    x, c = lax.axis_index("x"), lax.axis_index("c")
    depth, width = w_ref.shape[1], o_ref.shape[1]
    copies = []
    for at, slot in enumerate((0, 1, 7, 2, 6, 3, 5, 4)):
        copies.append(pltpu.make_async_copy(ring[at], a_ref.at[slot], sem.at[at]))
    turns = [x, x + NX - 1, x + 1, x + 2]
    for at in range(NZ):
        slot = turn_of(chunk, turns[at % NX] % NX, c if at < NX else 1 - c)
        copies.append(pltpu.make_async_copy(pieces[at], w_ref.at[slot], sem.at[NZ + at]))
    for copy in copies:
        copy.start()
    for copy in copies:
        copy.wait()
    whole = jnp.dot(
        jnp.concatenate([a_ref[k] for k in range(NZ)], axis=1),
        w_ref[...].reshape(NZ * depth, w_ref.shape[2]),
        preferred_element_type=F32,
    )
    o_ref[...] = whole[:, :width].astype(BF16)
    p_ref[...] = whole[:, width:].astype(BF16)


def base_product(chunk, ring, pieces, space, *deps):
    tokens, width = ring[0].shape
    depth, wide = pieces[0].shape

    def body(*refs):
        base_body(chunk, *refs)

    return pl.pallas_call(
        body,
        out_shape=[space((tokens, width), BF16)] * 2 + [jax.ShapeDtypeStruct((8, 128), F32)],
        in_specs=[ANY] * (2 * NZ + len(deps)),
        out_specs=[LOCAL] * 3,
        scratch_shapes=[
            pltpu.VMEM((NZ, tokens, width), BF16),
            pltpu.VMEM((NZ, depth, wide), BF16),
            pltpu.SemaphoreType.DMA((2 * NZ,)),
        ],
        compiler_params=params(),
        cost_estimate=cost(WEIGHT[chunk] * 2 * tokens * NZ * depth * wide, WEIGHT[chunk] * 4 * 1024 * 1024),
    )(*ring, *pieces, *deps)


def final_body(*refs):
    parts, (scale_ref, target_ref, back_ref, o_ref) = refs[:NY], refs[NY:]
    tokens = o_ref.shape[0]
    back = back_ref[...].reshape(GROUPS * CAP, back_ref.shape[2])
    step = 256
    for b in range(tokens // step):
        here = slice(b * step, (b + 1) * step)
        spot = lax.broadcasted_iota(jnp.int32, (GROUPS * CAP, step), 0).astype(F32)
        select = jnp.where(spot == target_ref[:1, here], 1.0, 0.0).astype(BF16)
        delta = lax.dot_general(select, back, TN, preferred_element_type=F32)
        summed = parts[0][here, :].astype(F32)
        for part in parts[1:]:
            summed += part[here, :].astype(F32)
        o_ref[here, :] = (summed * scale_ref[...] + delta).astype(BF16)


def final(parts, scale, target, back):
    tokens, width = parts[0].shape
    return pl.pallas_call(
        final_body,
        out_shape=jax.ShapeDtypeStruct((tokens, width), BF16),
        in_specs=[LOCAL] * (NY + 3),
        out_specs=LOCAL,
        compiler_params=params(),
        cost_estimate=cost(2 * GROUPS * CAP * tokens * width, 4 * 1024 * 1024),
    )(*parts, scale, target, back)


def shift(a, axis, by, size):
    return lax.ppermute(a, axis, [(i, (i + by) % size) for i in range(size)])


def pass_on(chunk, a):
    pairs = []
    for at in range(NX * NC * NZ):
        i, j, k = at // (NC * NZ), at // NZ % NC, at % NZ
        pairs.append((at, (i * NC + j) * NZ + (k + turn_of(chunk, i, j)) % NZ))
    return lax.ppermute(a, ("x", "c", "z"), pairs)


def on_device(rows, weights, scale, down_maps, up_maps, owner, slot):
    tokens, width = rows.shape
    first, second, send, target = start(
        owner.reshape(1, tokens), slot.reshape(1, tokens), rows, weights
    )
    owns = [pass_on(0, first), pass_on(1, second)]
    got = lax.all_to_all(send, ("x", "c"), 0, 0, tiled=True)
    r1, l1 = shift(rows, "z", 1, NZ), shift(rows, "z", -1, NZ)
    low_part, slots = down(got, down_maps.reshape(-1, width))
    lefts = [shift(own, "x", 1, NX) for own in owns]
    rights = [shift(own, "x", -1, NX) for own in owns]
    r2, l2 = shift(r1, "z", 1, NZ), shift(l1, "z", -1, NZ)
    low_part = lax.all_to_all(low_part, ("y", "z"), 0, 0, tiled=True)
    low_all, token = total(low_part)
    low = lax.all_to_all(low_all, ("y", "z"), 0, 0, tiled=True)
    r3, l3 = shift(r2, "z", 1, NZ), shift(l2, "z", -1, NZ)
    r4 = shift(r3, "z", 1, NZ)
    ring = [rows, r1, l1, r2, l2, r3, l3, r4]
    fars = [shift(lefts[0], "x", 1, NX), shift(rights[1], "x", -1, NX)]
    chunks = []
    for mine in zip(owns, lefts, rights, fars):
        chunks.append([*mine, *(shift(piece, "c", 1, NC) for piece in mine)])

    delta, token = up(low, slots, up_maps.reshape(-1, width))
    back = lax.all_to_all(delta, ("x", "c"), 0, 0, tiled=True)
    two, one, token = base_product(0, ring, chunks[0], pltpu.HBM, token)
    three, zero, _ = base_product(1, ring, chunks[1], pltpu.VMEM, token)
    parts = [zero, shift(two, "y", 2, NY), shift(one, "y", 1, NY), shift(three, "y", 3, NY)]
    return final(parts, scale.reshape(1, width), target, back)

def solution(mesh):
    fine = Mesh(mesh.devices.reshape(NX, NC, NY, NZ), ("x", "c", "y", "z"))
    grp, tp = ("x", "c"), ("y", "z")
    in_specs = (
        P(grp, tp),
        P(tp, None),
        P(tp),
        P(grp, None, tp),
        P(grp, None, tp),
        P(grp, None),
        P(grp),
    )
    return jax.shard_map(
        on_device, mesh=fine, in_specs=in_specs, out_specs=P(grp, tp), check_vma=False
    )
```

```python
import jax
import jax.numpy as jnp
from jax import lax
from jax.experimental import pallas as pl
from jax.experimental.pallas import tpu as pltpu
from jax.sharding import Mesh, PartitionSpec as P

NX, NC, NY, NZ = 4, 2, 4, 8
GROUPS = NX * NC
CAP = 128
EXTRA = 16
ROWS = CAP + EXTRA
RANK = 64
PARTS = 2
F32, BF16 = jnp.float32, jnp.bfloat16
NT = (((1,), (1,)), ((), ()))
TN = (((0,), (0,)), ((), ()))
LOCAL = pl.BlockSpec(memory_space=pltpu.VMEM)
REMOTE = pl.BlockSpec(memory_space=pltpu.HBM)
ANY = pl.BlockSpec(memory_space=pl.ANY)


def in_hbm(a):
    return pltpu.with_memory_space_constraint(a, pltpu.HBM)


def params(mib=12):
    return pltpu.CompilerParams(vmem_limit_bytes=mib * 1024 * 1024)


def cost(flops, nbytes):
    return pl.CostEstimate(flops=flops, bytes_accessed=nbytes, transcendentals=0)


def turn_of(chunk, x, c):
    return (x if chunk == 0 else x + 1 - 2 * (x % 2)) + NX * c


WEIGHT = (4, 4)
CHUNKS = ((2, 1), (3, 0))


def start_body(
    owner_ref, slot_ref, rows_ref, w_ref, first_ref, second_ref, send_ref, target_ref, sem
):
    x, c, y, z = (lax.axis_index(name) for name in ("x", "c", "y", "z"))
    width = rows_ref.shape[1]
    copies = []
    for chunk, out in enumerate((first_ref, second_ref)):
        column = (z + turn_of(chunk, x, c)) % NZ
        for at, by in enumerate(CHUNKS[chunk]):
            offset = pl.multiple_of(((y + by) % NY * NZ + column) * width, 256)
            copies.append(
                pltpu.make_async_copy(
                    w_ref.at[:, pl.ds(offset, width)],
                    out.at[:, pl.ds(at * width, width)],
                    sem.at[2 * chunk + at],
                )
            )
    for copy in copies:
        copy.start()

    tokens = rows_ref.shape[0]
    owner = owner_ref[...]
    member = lax.broadcasted_iota(jnp.int32, (GROUPS, tokens), 0) == owner
    before = lax.broadcasted_iota(jnp.int32, (tokens, tokens), 0) < lax.broadcasted_iota(
        jnp.int32, (tokens, tokens), 1
    )
    earlier = jnp.dot(
        member.astype(F32).astype(BF16), before.astype(F32).astype(BF16), preferred_element_type=F32
    )
    position = jnp.sum(jnp.where(member, earlier, 0.0), axis=0, keepdims=True)
    target = owner.astype(F32) * CAP + position
    target_ref[...] = jnp.broadcast_to(target, target_ref.shape)
    rows = rows_ref[...]
    slots = jnp.broadcast_to(slot_ref[...].astype(F32), (EXTRA, tokens)).astype(BF16)
    for g in range(GROUPS):
        spot = lax.broadcasted_iota(jnp.int32, (CAP, tokens), 0).astype(F32) + float(g * CAP)
        select = jnp.where(spot == target, 1.0, 0.0).astype(BF16)
        send_ref[g, :CAP, :] = jnp.dot(select, rows, preferred_element_type=F32).astype(BF16)
        sent = lax.dot_general(slots, select, NT, preferred_element_type=F32).astype(BF16)
        send_ref[g, CAP:, :CAP] = sent
        send_ref[g, CAP:, CAP:] = sent
    for copy in copies:
        copy.wait()


def start(owner, slot, rows, weights):
    tokens, width = rows.shape
    depth = weights.shape[0]
    return pl.pallas_call(
        start_body,
        out_shape=(
            pltpu.VMEM((depth, 2 * width), BF16),
            pltpu.VMEM((depth, 2 * width), BF16),
            pltpu.HBM((GROUPS, ROWS, width), BF16),
            jax.ShapeDtypeStruct((8, tokens), F32),
        ),
        in_specs=[LOCAL, LOCAL, LOCAL, REMOTE],
        out_specs=(LOCAL, LOCAL, LOCAL, LOCAL),
        scratch_shapes=[pltpu.SemaphoreType.DMA((4,))],
        compiler_params=params(),
        cost_estimate=cost(8 * (2 * GROUPS * CAP * tokens * width), 8 * (4 * GROUPS * ROWS * width)),
    )(in_hbm(owner), in_hbm(slot), in_hbm(rows), in_hbm(weights))


def fetch(source, target, sem, parts):
    size = source.shape[0] // parts
    copies = []
    for i in range(parts):
        here = pl.ds(i * size, size)
        copies.append(pltpu.make_async_copy(source.at[here], target.at[here], sem.at[i]))
    for copy in copies:
        copy.start()
    return copies


def down_body(got_ref, source_ref, *refs):
    low_ref, slot_ref, map_ref, total_ref, sem = refs[-5:]
    copies = fetch(source_ref, map_ref, sem, PARTS)
    slot = jnp.concatenate(
        [got_ref[g, CAP:, :CAP].astype(F32)[:1, :] for g in range(GROUPS)], axis=1
    )
    slot_ref[...] = jnp.broadcast_to(slot, slot_ref.shape)
    per = map_ref.shape[0] // PARTS // 256
    for p in range(PARTS):
        copies[p].wait()
        for b in range(GROUPS // 2):
            rows = jnp.concatenate([got_ref[2 * b, :CAP, :], got_ref[2 * b + 1, :CAP, :]], axis=0)
            columns = slice(2 * b * CAP, 2 * (b + 1) * CAP)
            here = slot[:, columns]
            total = total_ref[:, columns] if p else jnp.zeros((RANK, 2 * CAP), F32)
            for n in range(p * per, (p + 1) * per):
                product = lax.dot_general(
                    map_ref[n * 256 : (n + 1) * 256, :], rows, NT, preferred_element_type=F32
                )
                for j in range(256 // RANK):
                    part = product[RANK * j : RANK * (j + 1), :]
                    total = jnp.where(here == float(n * 256 // RANK + j), part, total)
            if p < PARTS - 1:
                total_ref[:, columns] = total
                continue
            for g in range(2):
                for i in range(RANK // 16):
                    low_ref[(2 * b + g) * (RANK // 16) + i] = total[
                        16 * i : 16 * (i + 1), g * CAP : (g + 1) * CAP
                    ]


def down(got, maps, *deps):
    rows, width = GROUPS * CAP, maps.shape[1]
    return pl.pallas_call(
        down_body,
        out_shape=(
            pltpu.HBM((NY * NZ, 16, CAP), F32),
            jax.ShapeDtypeStruct((8, rows), F32),
        ),
        in_specs=[LOCAL, REMOTE] + [ANY] * len(deps),
        out_specs=(LOCAL, LOCAL),
        scratch_shapes=[
            pltpu.VMEM(maps.shape, BF16),
            pltpu.VMEM((RANK, rows), F32),
            pltpu.SemaphoreType.DMA((PARTS,)),
        ],
        compiler_params=params(),
        cost_estimate=cost(30 * (2 * rows * maps.shape[0] * width), 30 * (2 * maps.shape[0] * width)),
    )(got, in_hbm(maps), *deps)


def total_body(parts_ref, *refs):
    o_ref, token_ref = refs[-2:]
    token_ref[...] = parts_ref[0, :8, :]
    whole = jnp.sum(parts_ref[...], axis=0).astype(BF16)
    o_ref[...] = jnp.broadcast_to(whole[None], o_ref.shape)


def total(parts, *deps):
    return pl.pallas_call(
        total_body,
        out_shape=(pltpu.HBM(parts.shape, BF16), jax.ShapeDtypeStruct((8, 128), F32)),
        in_specs=[LOCAL] + [ANY] * len(deps),
        out_specs=(LOCAL, LOCAL),
        compiler_params=params(4),
        cost_estimate=cost(30 * (parts.size), 30 * (6 * parts.size)),
    )(parts, *deps)


def up_body(low_ref, slot_ref, source_ref, *refs):
    o_ref, token_ref, map_ref, sem = refs[-4:]
    token_ref[...] = slot_ref[:, :128]
    copies = fetch(source_ref, map_ref, sem, PARTS)
    per = RANK // 16
    for b in range(GROUPS // 2):
        halves = [
            jnp.concatenate([low_ref[g * per + i].astype(F32) for i in range(per)], axis=0)
            for g in (2 * b, 2 * b + 1)
        ]
        low = jnp.concatenate(halves, axis=1)
        here = slot_ref[:1, 2 * b * CAP : 2 * (b + 1) * CAP]
        spread = jnp.concatenate(
            [
                jnp.where(here == float(a), low, 0.0).astype(BF16)
                for a in range(map_ref.shape[0] // RANK)
            ],
            axis=0,
        )
        if b == 0:
            for copy in copies:
                copy.wait()
        out = lax.dot_general(spread, map_ref[...], TN, preferred_element_type=F32).astype(BF16)
        o_ref[2 * b] = out[:CAP]
        o_ref[2 * b + 1] = out[CAP:]


def up(low, slots, maps, *deps):
    rows, width = GROUPS * CAP, maps.shape[1]
    return pl.pallas_call(
        up_body,
        out_shape=(
            pltpu.HBM((GROUPS, CAP, width), BF16),
            jax.ShapeDtypeStruct((8, 128), F32),
        ),
        in_specs=[LOCAL, LOCAL, REMOTE] + [ANY] * len(deps),
        out_specs=(LOCAL, LOCAL),
        scratch_shapes=[pltpu.VMEM(maps.shape, BF16), pltpu.SemaphoreType.DMA((PARTS,))],
        compiler_params=params(20),
        cost_estimate=cost(30 * (2 * rows * maps.shape[0] * width), 30 * (2 * maps.shape[0] * width)),
    )(low, slots, in_hbm(maps), *deps)


def base_body(chunk, *refs):
    ring, pieces = refs[:NZ], refs[NZ : 2 * NZ]
    token_ref, a_ref, w_ref, sem = refs[-4:]
    token_ref[...] = jnp.zeros_like(token_ref)
    x, c = lax.axis_index("x"), lax.axis_index("c")
    depth, width = w_ref.shape[1], ring[0].shape[1]
    copies = []
    for at, slot in enumerate((0, 1, 7, 2, 6, 3, 5, 4)):
        copies.append(pltpu.make_async_copy(ring[at], a_ref.at[slot], sem.at[at]))
    turns = [x, x + NX - 1, x + 1, x + 2]
    for at in range(NZ):
        slot = turn_of(chunk, turns[at % NX] % NX, c if at < NX else 1 - c)
        copies.append(pltpu.make_async_copy(pieces[at], w_ref.at[slot], sem.at[NZ + at]))
    for copy in copies:
        copy.start()
    for copy in copies:
        copy.wait()
    whole = jnp.dot(
        jnp.concatenate([a_ref[k] for k in range(NZ)], axis=1),
        w_ref[...].reshape(NZ * depth, w_ref.shape[2]),
        preferred_element_type=F32,
    )
    whole = whole.astype(BF16)
    if chunk == 0:
        top_ref, bottom_ref, p_ref = refs[-7:-4]
        half = whole.shape[0] // 2
        top_ref[...] = whole[:half, :width]
        bottom_ref[...] = whole[half:, :width]
    else:
        o_ref, p_ref = refs[-6:-4]
        o_ref[...] = whole[:, :width]
    p_ref[...] = whole[:, width:]


def base_product(chunk, ring, pieces, space, *deps):
    tokens, width = ring[0].shape
    depth, wide = pieces[0].shape

    def body(*refs):
        base_body(chunk, *refs)

    block, half = space((tokens, width), BF16), space((tokens // 2, width), BF16)
    outs = [half, half, block] if chunk == 0 else [block, block]
    return pl.pallas_call(
        body,
        out_shape=[*outs, jax.ShapeDtypeStruct((8, 128), F32)],
        in_specs=[ANY] * (2 * NZ + len(deps)),
        out_specs=[LOCAL] * (len(outs) + 1),
        scratch_shapes=[
            pltpu.VMEM((NZ, tokens, width), BF16),
            pltpu.VMEM((NZ, depth, wide), BF16),
            pltpu.SemaphoreType.DMA((2 * NZ,)),
        ],
        compiler_params=params(),
        cost_estimate=cost(WEIGHT[chunk] * 2 * tokens * NZ * depth * wide, WEIGHT[chunk] * 4 * 1024 * 1024),
    )(*ring, *pieces, *deps)


def final_body(*refs):
    parts, halves, (scale_ref, target_ref, back_ref, o_ref) = refs[:3], refs[3:5], refs[5:]
    tokens = o_ref.shape[0]
    back = back_ref[...].reshape(GROUPS * CAP, back_ref.shape[2])
    step = tokens // 2
    for b in range(tokens // step):
        here = slice(b * step, (b + 1) * step)
        spot = lax.broadcasted_iota(jnp.int32, (GROUPS * CAP, step), 0).astype(F32)
        select = jnp.where(spot == target_ref[:1, here], 1.0, 0.0).astype(BF16)
        delta = lax.dot_general(select, back, TN, preferred_element_type=F32)
        summed = halves[b][...].astype(F32)
        for part in parts:
            summed += part[here, :].astype(F32)
        o_ref[here, :] = (summed * scale_ref[...] + delta).astype(BF16)


def final(parts, scale, target, back):
    tokens, width = parts[0].shape
    return pl.pallas_call(
        final_body,
        out_shape=jax.ShapeDtypeStruct((tokens, width), BF16),
        in_specs=[LOCAL] * (NY + 4),
        out_specs=LOCAL,
        compiler_params=params(),
        cost_estimate=cost(2 * GROUPS * CAP * tokens * width, 4 * 1024 * 1024),
    )(*parts, scale, target, back)


def shift(a, axis, by, size):
    return lax.ppermute(a, axis, [(i, (i + by) % size) for i in range(size)])


def pass_on(chunk, a):
    pairs = []
    for at in range(NX * NC * NZ):
        i, j, k = at // (NC * NZ), at // NZ % NC, at % NZ
        pairs.append((at, (i * NC + j) * NZ + (k + turn_of(chunk, i, j)) % NZ))
    return lax.ppermute(a, ("x", "c", "z"), pairs)


def on_device(rows, weights, scale, down_maps, up_maps, owner, slot):
    tokens, width = rows.shape
    first, second, send, target = start(
        owner.reshape(1, tokens), slot.reshape(1, tokens), rows, weights
    )
    owns = [pass_on(0, first), pass_on(1, second)]
    got = lax.all_to_all(send, ("x", "c"), 0, 0, tiled=True)
    r1, l1 = shift(rows, "z", 1, NZ), shift(rows, "z", -1, NZ)
    low_part, slots = down(got, down_maps.reshape(-1, width))
    lefts = [shift(own, "x", 1, NX) for own in owns]
    rights = [shift(own, "x", -1, NX) for own in owns]
    r2, l2 = shift(r1, "z", 1, NZ), shift(l1, "z", -1, NZ)
    low_part = lax.all_to_all(low_part, ("y", "z"), 0, 0, tiled=True)
    low_all, token = total(low_part)
    low = lax.all_to_all(low_all, ("y", "z"), 0, 0, tiled=True)
    r3, l3 = shift(r2, "z", 1, NZ), shift(l2, "z", -1, NZ)
    r4 = shift(r3, "z", 1, NZ)
    ring = [rows, r1, l1, r2, l2, r3, l3, r4]
    fars = [shift(lefts[0], "x", 1, NX), shift(rights[1], "x", -1, NX)]
    chunks = []
    for mine in zip(owns, lefts, rights, fars):
        chunks.append([*mine, *(shift(piece, "c", 1, NC) for piece in mine)])

    delta, token = up(low, slots, up_maps.reshape(-1, width))
    back = lax.all_to_all(delta, ("x", "c"), 0, 0, tiled=True)
    top, bottom, one, token = base_product(0, ring, chunks[0], pltpu.HBM, token)
    three, zero, _ = base_product(1, ring, chunks[1], pltpu.VMEM, token)
    bottom = shift(shift(bottom, "y", 3, NY), "y", 3, NY)
    parts = [zero, shift(one, "y", 1, NY), shift(three, "y", 3, NY), shift(top, "y", 2, NY), bottom]
    return final(parts, scale.reshape(1, width), target, back)

def solution(mesh):
    fine = Mesh(mesh.devices.reshape(NX, NC, NY, NZ), ("x", "c", "y", "z"))
    grp, tp = ("x", "c"), ("y", "z")
    in_specs = (
        P(grp, tp),
        P(tp, None),
        P(tp),
        P(grp, None, tp),
        P(grp, None, tp),
        P(grp, None),
        P(grp),
    )
    return jax.shard_map(
        on_device, mesh=fine, in_specs=in_specs, out_specs=P(grp, tp), check_vma=False
    )
```

```python
import jax
import jax.numpy as jnp
from jax import lax
from jax.experimental import pallas as pl
from jax.experimental.pallas import tpu as pltpu
from jax.sharding import Mesh, PartitionSpec as P

NX, NC, NY, NZ = 4, 2, 4, 8
GROUPS = NX * NC
CAP = 128
EXTRA = 16
ROWS = CAP + EXTRA
RANK = 64
PARTS = 2
F32, BF16 = jnp.float32, jnp.bfloat16
NT = (((1,), (1,)), ((), ()))
TN = (((0,), (0,)), ((), ()))
LOCAL = pl.BlockSpec(memory_space=pltpu.VMEM)
REMOTE = pl.BlockSpec(memory_space=pltpu.HBM)
ANY = pl.BlockSpec(memory_space=pl.ANY)


def in_hbm(a):
    return pltpu.with_memory_space_constraint(a, pltpu.HBM)


def params(mib=12):
    return pltpu.CompilerParams(vmem_limit_bytes=mib * 1024 * 1024)


def cost(flops, nbytes):
    return pl.CostEstimate(flops=flops, bytes_accessed=nbytes, transcendentals=0)


def turn_of(chunk, x, c):
    return (x if chunk == 0 else x + 1 - 2 * (x % 2)) + NX * c


WEIGHT = (4, 4)
CHUNKS = ((2, 1), (3, 0))


def start_body(
    owner_ref, slot_ref, rows_ref, w_ref, first_ref, second_ref, send_ref, target_ref, sem
):
    x, c, y, z = (lax.axis_index(name) for name in ("x", "c", "y", "z"))
    width = rows_ref.shape[1]
    copies = []
    for chunk, out in enumerate((first_ref, second_ref)):
        column = (z + turn_of(chunk, x, c)) % NZ
        for at, by in enumerate(CHUNKS[chunk]):
            offset = pl.multiple_of(((y + by) % NY * NZ + column) * width, 256)
            copies.append(
                pltpu.make_async_copy(
                    w_ref.at[:, pl.ds(offset, width)],
                    out.at[:, pl.ds(at * width, width)],
                    sem.at[2 * chunk + at],
                )
            )
    for copy in copies:
        copy.start()

    tokens = rows_ref.shape[0]
    owner = owner_ref[...]
    member = lax.broadcasted_iota(jnp.int32, (GROUPS, tokens), 0) == owner
    before = lax.broadcasted_iota(jnp.int32, (tokens, tokens), 0) < lax.broadcasted_iota(
        jnp.int32, (tokens, tokens), 1
    )
    earlier = jnp.dot(
        member.astype(F32).astype(BF16), before.astype(F32).astype(BF16), preferred_element_type=F32
    )
    position = jnp.sum(jnp.where(member, earlier, 0.0), axis=0, keepdims=True)
    target = owner.astype(F32) * CAP + position
    target_ref[...] = jnp.broadcast_to(target, target_ref.shape)
    rows = rows_ref[...]
    slots = jnp.broadcast_to(slot_ref[...].astype(F32), (EXTRA, tokens)).astype(BF16)
    for g in range(GROUPS):
        spot = lax.broadcasted_iota(jnp.int32, (CAP, tokens), 0).astype(F32) + float(g * CAP)
        select = jnp.where(spot == target, 1.0, 0.0).astype(BF16)
        send_ref[g, :CAP, :] = jnp.dot(select, rows, preferred_element_type=F32).astype(BF16)
        sent = lax.dot_general(slots, select, NT, preferred_element_type=F32).astype(BF16)
        send_ref[g, CAP:, :CAP] = sent
        send_ref[g, CAP:, CAP:] = sent
    for copy in copies:
        copy.wait()


def start(owner, slot, rows, weights):
    tokens, width = rows.shape
    depth = weights.shape[0]
    return pl.pallas_call(
        start_body,
        out_shape=(
            pltpu.VMEM((depth, 2 * width), BF16),
            pltpu.VMEM((depth, 2 * width), BF16),
            pltpu.HBM((GROUPS, ROWS, width), BF16),
            jax.ShapeDtypeStruct((8, tokens), F32),
        ),
        in_specs=[LOCAL, LOCAL, LOCAL, REMOTE],
        out_specs=(LOCAL, LOCAL, LOCAL, LOCAL),
        scratch_shapes=[pltpu.SemaphoreType.DMA((4,))],
        compiler_params=params(),
        cost_estimate=cost(8 * (2 * GROUPS * CAP * tokens * width), 8 * (4 * GROUPS * ROWS * width)),
    )(in_hbm(owner), in_hbm(slot), in_hbm(rows), in_hbm(weights))


def fetch(source, target, sem, parts):
    size = source.shape[0] // parts
    copies = []
    for i in range(parts):
        here = pl.ds(i * size, size)
        copies.append(pltpu.make_async_copy(source.at[here], target.at[here], sem.at[i]))
    for copy in copies:
        copy.start()
    return copies


def down_body(got_ref, source_ref, *refs):
    low_ref, slot_ref, map_ref, total_ref, sem = refs[-5:]
    copies = fetch(source_ref, map_ref, sem, PARTS)
    slot = jnp.concatenate(
        [got_ref[g, CAP:, :CAP].astype(F32)[:1, :] for g in range(GROUPS)], axis=1
    )
    slot_ref[...] = jnp.broadcast_to(slot, slot_ref.shape)
    per = map_ref.shape[0] // PARTS // 256
    for p in range(PARTS):
        copies[p].wait()
        for b in range(GROUPS // 2):
            rows = jnp.concatenate([got_ref[2 * b, :CAP, :], got_ref[2 * b + 1, :CAP, :]], axis=0)
            columns = slice(2 * b * CAP, 2 * (b + 1) * CAP)
            here = slot[:, columns]
            total = total_ref[:, columns] if p else jnp.zeros((RANK, 2 * CAP), F32)
            for n in range(p * per, (p + 1) * per):
                product = lax.dot_general(
                    map_ref[n * 256 : (n + 1) * 256, :], rows, NT, preferred_element_type=F32
                )
                for j in range(256 // RANK):
                    part = product[RANK * j : RANK * (j + 1), :]
                    total = jnp.where(here == float(n * 256 // RANK + j), part, total)
            if p < PARTS - 1:
                total_ref[:, columns] = total
                continue
            for g in range(2):
                for i in range(RANK // 16):
                    low_ref[(2 * b + g) * (RANK // 16) + i] = total[
                        16 * i : 16 * (i + 1), g * CAP : (g + 1) * CAP
                    ].astype(BF16)


def down(got, maps, *deps):
    rows, width = GROUPS * CAP, maps.shape[1]
    return pl.pallas_call(
        down_body,
        out_shape=(
            pltpu.HBM((NY * NZ, 16, CAP), BF16),
            jax.ShapeDtypeStruct((8, rows), F32),
        ),
        in_specs=[LOCAL, REMOTE] + [ANY] * len(deps),
        out_specs=(LOCAL, LOCAL),
        scratch_shapes=[
            pltpu.VMEM(maps.shape, BF16),
            pltpu.VMEM((RANK, rows), F32),
            pltpu.SemaphoreType.DMA((PARTS,)),
        ],
        compiler_params=params(),
        cost_estimate=cost(30 * (2 * rows * maps.shape[0] * width), 30 * (2 * maps.shape[0] * width)),
    )(got, in_hbm(maps), *deps)


def total_body(parts_ref, *refs):
    o_ref, token_ref = refs[-2:]
    token_ref[...] = parts_ref[0].astype(F32)[:8, :]
    whole = jnp.sum(parts_ref[...].astype(F32), axis=0).astype(BF16)
    o_ref[...] = jnp.broadcast_to(whole[None], o_ref.shape)


def total(parts, *deps):
    return pl.pallas_call(
        total_body,
        out_shape=(pltpu.HBM(parts.shape, BF16), jax.ShapeDtypeStruct((8, 128), F32)),
        in_specs=[LOCAL] + [ANY] * len(deps),
        out_specs=(LOCAL, LOCAL),
        compiler_params=params(4),
        cost_estimate=cost(30 * (parts.size), 30 * (6 * parts.size)),
    )(parts, *deps)


def up_body(low_ref, slot_ref, source_ref, *refs):
    o_ref, token_ref, map_ref, sem = refs[-4:]
    token_ref[...] = slot_ref[:, :128]
    copies = fetch(source_ref, map_ref, sem, PARTS)
    per = RANK // 16
    for b in range(GROUPS // 2):
        halves = [
            jnp.concatenate([low_ref[g * per + i].astype(F32) for i in range(per)], axis=0)
            for g in (2 * b, 2 * b + 1)
        ]
        low = jnp.concatenate(halves, axis=1)
        here = slot_ref[:1, 2 * b * CAP : 2 * (b + 1) * CAP]
        spread = jnp.concatenate(
            [
                jnp.where(here == float(a), low, 0.0).astype(BF16)
                for a in range(map_ref.shape[0] // RANK)
            ],
            axis=0,
        )
        if b == 0:
            for copy in copies:
                copy.wait()
        out = lax.dot_general(spread, map_ref[...], TN, preferred_element_type=F32).astype(BF16)
        o_ref[2 * b] = out[:CAP]
        o_ref[2 * b + 1] = out[CAP:]


def up(low, slots, maps, *deps):
    rows, width = GROUPS * CAP, maps.shape[1]
    return pl.pallas_call(
        up_body,
        out_shape=(
            pltpu.HBM((GROUPS, CAP, width), BF16),
            jax.ShapeDtypeStruct((8, 128), F32),
        ),
        in_specs=[LOCAL, LOCAL, REMOTE] + [ANY] * len(deps),
        out_specs=(LOCAL, LOCAL),
        scratch_shapes=[pltpu.VMEM(maps.shape, BF16), pltpu.SemaphoreType.DMA((PARTS,))],
        compiler_params=params(20),
        cost_estimate=cost(30 * (2 * rows * maps.shape[0] * width), 30 * (2 * maps.shape[0] * width)),
    )(low, slots, in_hbm(maps), *deps)


def base_body(chunk, *refs):
    ring, pieces = refs[:NZ], refs[NZ : 2 * NZ]
    token_ref, a_ref, w_ref, sem = refs[-4:]
    token_ref[...] = jnp.zeros_like(token_ref)
    x, c = lax.axis_index("x"), lax.axis_index("c")
    depth, width = w_ref.shape[1], ring[0].shape[1]
    copies = []
    for at, slot in enumerate((0, 1, 7, 2, 6, 3, 5, 4)):
        copies.append(pltpu.make_async_copy(ring[at], a_ref.at[slot], sem.at[at]))
    turns = [x, x + NX - 1, x + 1, x + 2]
    for at in range(NZ):
        slot = turn_of(chunk, turns[at % NX] % NX, c if at < NX else 1 - c)
        copies.append(pltpu.make_async_copy(pieces[at], w_ref.at[slot], sem.at[NZ + at]))
    for copy in copies:
        copy.start()
    for copy in copies:
        copy.wait()
    whole = jnp.dot(
        jnp.concatenate([a_ref[k] for k in range(NZ)], axis=1),
        w_ref[...].reshape(NZ * depth, w_ref.shape[2]),
        preferred_element_type=F32,
    )
    whole = whole.astype(BF16)
    if chunk == 0:
        top_ref, bottom_ref, p_ref = refs[-7:-4]
        half = whole.shape[0] // 2
        top_ref[...] = whole[:half, :width]
        bottom_ref[...] = whole[half:, :width]
    else:
        o_ref, p_ref = refs[-6:-4]
        o_ref[...] = whole[:, :width]
    p_ref[...] = whole[:, width:]


def base_product(chunk, ring, pieces, space, *deps):
    tokens, width = ring[0].shape
    depth, wide = pieces[0].shape

    def body(*refs):
        base_body(chunk, *refs)

    block, half = space((tokens, width), BF16), space((tokens // 2, width), BF16)
    outs = [half, half, block] if chunk == 0 else [block, block]
    return pl.pallas_call(
        body,
        out_shape=[*outs, jax.ShapeDtypeStruct((8, 128), F32)],
        in_specs=[ANY] * (2 * NZ + len(deps)),
        out_specs=[LOCAL] * (len(outs) + 1),
        scratch_shapes=[
            pltpu.VMEM((NZ, tokens, width), BF16),
            pltpu.VMEM((NZ, depth, wide), BF16),
            pltpu.SemaphoreType.DMA((2 * NZ,)),
        ],
        compiler_params=params(),
        cost_estimate=cost(WEIGHT[chunk] * 2 * tokens * NZ * depth * wide, WEIGHT[chunk] * 4 * 1024 * 1024),
    )(*ring, *pieces, *deps)


def final_body(*refs):
    parts, halves, (scale_ref, target_ref, back_ref, o_ref) = refs[:3], refs[3:5], refs[5:]
    tokens = o_ref.shape[0]
    back = back_ref[...].reshape(GROUPS * CAP, back_ref.shape[2])
    step = tokens // 2
    for b in range(tokens // step):
        here = slice(b * step, (b + 1) * step)
        spot = lax.broadcasted_iota(jnp.int32, (GROUPS * CAP, step), 0).astype(F32)
        select = jnp.where(spot == target_ref[:1, here], 1.0, 0.0).astype(BF16)
        delta = lax.dot_general(select, back, TN, preferred_element_type=F32)
        summed = halves[b][...].astype(F32)
        for part in parts:
            summed += part[here, :].astype(F32)
        o_ref[here, :] = (summed * scale_ref[...] + delta).astype(BF16)


def final(parts, scale, target, back):
    tokens, width = parts[0].shape
    return pl.pallas_call(
        final_body,
        out_shape=jax.ShapeDtypeStruct((tokens, width), BF16),
        in_specs=[LOCAL] * (NY + 4),
        out_specs=LOCAL,
        compiler_params=params(),
        cost_estimate=cost(2 * GROUPS * CAP * tokens * width, 4 * 1024 * 1024),
    )(*parts, scale, target, back)


def shift(a, axis, by, size):
    return lax.ppermute(a, axis, [(i, (i + by) % size) for i in range(size)])


def pass_on(chunk, a):
    pairs = []
    for at in range(NX * NC * NZ):
        i, j, k = at // (NC * NZ), at // NZ % NC, at % NZ
        pairs.append((at, (i * NC + j) * NZ + (k + turn_of(chunk, i, j)) % NZ))
    return lax.ppermute(a, ("x", "c", "z"), pairs)


def on_device(rows, weights, scale, down_maps, up_maps, owner, slot):
    tokens, width = rows.shape
    first, second, send, target = start(
        owner.reshape(1, tokens), slot.reshape(1, tokens), rows, weights
    )
    owns = [pass_on(0, first), pass_on(1, second)]
    got = lax.all_to_all(send, ("x", "c"), 0, 0, tiled=True)
    r1, l1 = shift(rows, "z", 1, NZ), shift(rows, "z", -1, NZ)
    low_part, slots = down(got, down_maps.reshape(-1, width))
    lefts = [shift(own, "x", 1, NX) for own in owns]
    rights = [shift(own, "x", -1, NX) for own in owns]
    r2, l2 = shift(r1, "z", 1, NZ), shift(l1, "z", -1, NZ)
    low_part = lax.all_to_all(low_part, ("y", "z"), 0, 0, tiled=True)
    low_all, token = total(low_part)
    low = lax.all_to_all(low_all, ("y", "z"), 0, 0, tiled=True)
    r3, l3 = shift(r2, "z", 1, NZ), shift(l2, "z", -1, NZ)
    r4 = shift(r3, "z", 1, NZ)
    ring = [rows, r1, l1, r2, l2, r3, l3, r4]
    fars = [shift(lefts[0], "x", 1, NX), shift(rights[1], "x", -1, NX)]
    chunks = []
    for mine in zip(owns, lefts, rights, fars):
        chunks.append([*mine, *(shift(piece, "c", 1, NC) for piece in mine)])

    delta, token = up(low, slots, up_maps.reshape(-1, width))
    back = lax.all_to_all(delta, ("x", "c"), 0, 0, tiled=True)
    top, bottom, one, token = base_product(0, ring, chunks[0], pltpu.HBM, token)
    three, zero, _ = base_product(1, ring, chunks[1], pltpu.VMEM, token)
    bottom = shift(shift(bottom, "y", 3, NY), "y", 3, NY)
    parts = [zero, shift(one, "y", 1, NY), shift(three, "y", 3, NY), shift(top, "y", 2, NY), bottom]
    return final(parts, scale.reshape(1, width), target, back)

def solution(mesh):
    fine = Mesh(mesh.devices.reshape(NX, NC, NY, NZ), ("x", "c", "y", "z"))
    grp, tp = ("x", "c"), ("y", "z")
    in_specs = (
        P(grp, tp),
        P(tp, None),
        P(tp),
        P(grp, None, tp),
        P(grp, None, tp),
        P(grp, None),
        P(grp),
    )
    return jax.shard_map(
        on_device, mesh=fine, in_specs=in_specs, out_specs=P(grp, tp), check_vma=False
    )
```
